512 devices in a mesh: region: 8 (over z), tile: 64 (over y, x, core).
Axes of the slice: x: 4, y: 8, z: 8, core: 2. Of those that a mesh axis runs over, the one named last changes fastest.
Arguments:
- anomalies: bfloat16 [131072, 4096], P(('region', 'tile')), may hold values from -20 to 20
- station_count: int32 [512], P(('region', 'tile')), may hold values from 32 to 256, as said below
- composite_of: int32 [131072], P(('region', 'tile')), may hold values from 0 to 127
Outputs:
- near_corr: float32 [131072, 512], P(('region', 'tile'))
- comp_corr: float32 [131072, 1024], P(('region', 'tile'))
The draws below stay inside these ranges and needn't reach their ends.
Inputs may be any that keep to these rules, and one draw needn't show every extreme that they name: `station_count`: each tile's live stations fill its first slots; some tile is full in every draw.
All inputs are finite; a program needn't handle non-finite values.
Results may differ from the reference program's by a relative error of at most 0.0048.
Values may be sent and summed in bfloat16 or wider, within the bound.
No kernel may reach another device: no remote copies, remote signals or barrier semaphores. Data moves between devices by JAX's collectives and lax.ppermute only.
A program may use at most 64 MiB of HBM per device.

```python
import jax
import jax.numpy as jnp
from jax import lax

CAP = 256
HOURS = 4096
COMPOSITES = 1024
SLOTS = 131072
COMP_REG = 128
N_REGION = 8
N_TILE = 64


def draw_anomalies(key, part):
    key = jax.random.fold_in(key, 11)
    keys = jax.random.split(key, 4)
    offsets = jax.random.uniform(keys[0], (SLOTS, 1), jnp.float32, -5.0, 5.0)
    scales = jnp.exp(jax.random.uniform(keys[1], (SLOTS, 1), jnp.float32, jnp.log(0.3), jnp.log(3.0)))
    noise = jnp.clip(jax.random.normal(keys[3], (SLOTS, HOURS), jnp.float32), -4.0, 4.0)
    values = offsets + scales * noise
    return values.astype(jnp.bfloat16)


def draw_station_count(key, part):
    key = jax.random.fold_in(key, 23)
    keys = jax.random.split(key, 2)
    tiles = SLOTS // CAP
    lowest = CAP // 8
    ranks = jax.random.randint(keys[0], (tiles,), 0, 64)
    counts = lowest + (CAP - lowest) * ranks * ranks * ranks // (63 * 63 * 63)
    full = jax.random.randint(keys[1], (), 0, tiles)
    return counts.at[full].set(CAP).astype(jnp.int32)


def set_ends(drawn, own_key, low, largest):
    longest = drawn.shape.index(max(drawn.shape))
    spots = []
    for shift in (0, 1):
        where = [jax.random.randint(jax.random.fold_in(own_key, axis), (), 0, length) for axis, length in enumerate(drawn.shape)]
        where[longest] = (where[longest] + shift) % drawn.shape[longest]
        spots.append(tuple(where))
    return drawn.at[spots[0]].set(low).at[spots[1]].set(largest)


def setup_inputs(seed: int = 0) -> dict:
    key_of = jax.random.split(jax.random.key(seed), 4)
    anomalies = draw_anomalies(jax.random.fold_in(key_of[3], 71), 0)
    station_count = draw_station_count(jax.random.fold_in(key_of[3], 71), 0)
    composite_of = set_ends(jax.random.randint(key_of[2], (SLOTS,), 0, COMP_REG), jax.random.fold_in(key_of[2], 1), 0, COMP_REG - 1).astype(jnp.int32)
    return {"anomalies": anomalies, "station_count": station_count, "composite_of": composite_of}


def normalize(rows):
    values = rows.astype(jnp.float32)
    center = values - lax.optimization_barrier(jnp.mean(values, axis=1, keepdims=True))
    return center * lax.rsqrt(lax.optimization_barrier(jnp.mean(center * center, axis=1, keepdims=True)) + 1e-05)

def cross(left, right):
    return lax.dot_general(left, right, (((1,), (1,)), ((), ())), preferred_element_type=jnp.float32) * (1.0 / HOURS)

def reference(anomalies, station_count, composite_of):
    tiles = N_REGION * N_TILE
    blocks = anomalies.reshape(tiles, CAP, HOURS)
    live = (jnp.arange(CAP)[None, :] < station_count[:, None]).astype(jnp.float32)

    def prepare(item):
        rows, alive = item
        return (normalize(rows) * alive[:, None]).astype(jnp.bfloat16)
    zed = lax.map(prepare, (blocks, live))
    region_rows = zed.reshape(N_REGION, N_TILE * CAP, HOURS)
    region_ids = composite_of.reshape(N_REGION, N_TILE * CAP)

    def region_sum(item):
        rows, ids = item
        onehot = (ids[None, :] == jnp.arange(COMP_REG)[:, None]).astype(jnp.bfloat16)
        return jnp.dot(onehot, rows, preferred_element_type=jnp.float32)
    sums = lax.map(region_sum, (region_rows, region_ids))
    comps = normalize(sums.reshape(COMPOSITES, HOURS)).astype(jnp.bfloat16)
    comp_corr = lax.map(lambda rows: cross(rows, comps), zed).reshape(SLOTS, COMPOSITES)
    grid = zed.reshape(N_REGION, N_TILE, CAP, HOURS)
    blank = jnp.zeros((N_REGION, 1, CAP, HOURS), jnp.bfloat16)
    before = jnp.concatenate([blank, grid[:, :-1]], axis=1).reshape(tiles, CAP, HOURS)
    after = jnp.concatenate([grid[:, 1:], blank], axis=1).reshape(tiles, CAP, HOURS)

    def pair_block(item):
        rows, prev_rows, next_rows = item
        return jnp.concatenate([cross(rows, prev_rows), cross(rows, next_rows)], axis=1)
    near_corr = lax.map(pair_block, (zed, before, after)).reshape(SLOTS, 2 * CAP)
    return (near_corr, comp_corr)
```

```python
import functools

import jax
import jax.numpy as jnp
from jax import lax
from jax.experimental import pallas as pl
from jax.experimental.pallas import tpu as pltpu
from jax.sharding import Mesh, PartitionSpec as P

HOURS = 4096
SLOTS = 256
COMP_REG = 128
HALF = COMP_REG // 2
EPS = 1e-05
CHUNK = 512
NCHUNK = HOURS // CHUNK
ROWS = 32
F32 = jnp.float32
BF16 = jnp.bfloat16
SMEM = pl.BlockSpec(memory_space=pltpu.SMEM)
NT = (((1,), (1,)), ((), ()))


def params(mib):
    return pltpu.CompilerParams(vmem_limit_bytes=mib << 20)


VMEM = pl.BlockSpec(memory_space=pltpu.VMEM)
HBM = pl.BlockSpec(memory_space=pltpu.HBM)


def zed_kernel(count, core, ids, x, zed, edge, own, theirs, held, sems):
    steps = SLOTS // ROWS
    rows_of = lambda step: pl.ds(step * ROWS, ROWS)
    copies = [
        pltpu.make_async_copy(x.at[rows_of(step)], held.at[rows_of(step)], sems.at[step]) for step in range(steps)
    ]
    for copy in copies:
        copy.start()
    for step, copy in enumerate(copies):
        copy.wait()
        values = held[rows_of(step), :].astype(F32)
        center = values - jnp.mean(values, axis=1, keepdims=True)
        scale = lax.rsqrt(jnp.mean(center * center, axis=1, keepdims=True) + EPS)
        slot = step * ROWS + lax.broadcasted_iota(jnp.int32, (ROWS, 1), 0)
        live = (slot < count[0]).astype(F32)
        rows = (center * scale * live).astype(BF16)
        zed[rows_of(step), :] = rows
        edge[rows_of(step), :] = jnp.where(core[0] == 0, rows[:, : HOURS // 2], rows[:, HOURS // 2 :])

    index = lax.broadcasted_iota(jnp.int32, (COMP_REG, SLOTS), 0)
    index = (index + HALF * core[0]) & (COMP_REG - 1)
    hot = (ids[...] == index).astype(F32).astype(BF16)
    for k in range(NCHUNK):
        part = jnp.dot(hot, zed[:, k * CHUNK : (k + 1) * CHUNK], preferred_element_type=F32)
        own[k] = part[:HALF]
        theirs[k] = part[HALF:].astype(BF16)


def make_zed(count, core, ids, x):
    block = (NCHUNK, HALF, CHUNK)
    return pl.pallas_call(
        zed_kernel,
        in_specs=[SMEM, SMEM, VMEM, HBM],
        out_specs=[VMEM] * 4,
        out_shape=[
            jax.ShapeDtypeStruct((SLOTS, HOURS), BF16),
            jax.ShapeDtypeStruct((SLOTS, HOURS // 2), BF16),
            jax.ShapeDtypeStruct(block, F32),
            jax.ShapeDtypeStruct(block, BF16),
        ],
        scratch_shapes=[pltpu.VMEM((SLOTS, HOURS), BF16), pltpu.SemaphoreType.DMA((SLOTS // ROWS,))],
        compiler_params=params(24),
        cost_estimate=pl.CostEstimate(flops=300_000_000, bytes_accessed=6 << 20, transcendentals=0),
        name="normalize_and_sum",
    )(count, core, ids, x)


def lane_sums(block):
    wide = block[:, :128]
    for k in range(1, block.shape[1] // 128):
        wide = wide + block[:, k * 128 : (k + 1) * 128]
    return wide


def near_kernel(core, zed, other, halo, same, mine, theirs, zsum, osum, wide):
    z = zed[...]
    same[...] = lax.dot_general(z, other[...], NT, preferred_element_type=F32) * (1.0 / HOURS)

    @pl.when(core[0] == 0)
    def _():
        half = zed[:, HOURS // 2 :]
        mine[...] = lax.dot_general(half, halo[...], NT, preferred_element_type=F32)
        theirs[...] = lax.dot_general(halo[...], half, NT, preferred_element_type=F32)

    @pl.when(core[0] != 0)
    def _():
        half = zed[:, : HOURS // 2]
        mine[...] = lax.dot_general(half, halo[...], NT, preferred_element_type=F32)
        theirs[...] = lax.dot_general(halo[...], half, NT, preferred_element_type=F32)

    for rows, out in ((zed, zsum), (other, osum)):
        wide[...] = lane_sums(rows[:, :CHUNK].astype(F32))
        for k in range(1, NCHUNK):
            wide[...] += lane_sums(rows[:, k * CHUNK : (k + 1) * CHUNK].astype(F32))
        out[...] = jnp.broadcast_to(jnp.sum(wide[...], axis=1, keepdims=True), out.shape)


def make_near(place, zed, other, halo):
    square = jax.ShapeDtypeStruct((SLOTS, SLOTS), F32)
    return pl.pallas_call(
        near_kernel,
        in_specs=[SMEM, VMEM, VMEM, VMEM],
        out_specs=[VMEM] * 5,
        out_shape=[square] * 3 + [jax.ShapeDtypeStruct((SLOTS, 128), F32)] * 2,
        scratch_shapes=[pltpu.VMEM((SLOTS, 128), F32)],
        compiler_params=params(16),
        cost_estimate=pl.CostEstimate(flops=1_073_741_824, bytes_accessed=6 << 20, transcendentals=0),
        name="neighbour_correlation",
    )(place, zed, other, halo)


def near_sum_kernel(core, same, mine, got, near):
    at = pl.multiple_of(core[0] * SLOTS, SLOTS)
    near[:, pl.ds(at, SLOTS)] = (mine[...] + got[...]) * (1.0 / HOURS)
    near[:, pl.ds(SLOTS - at, SLOTS)] = same[...]


def near_sum(place, same, mine, got):
    return pl.pallas_call(
        near_sum_kernel,
        in_specs=[SMEM, VMEM, VMEM, VMEM],
        out_specs=VMEM,
        out_shape=jax.ShapeDtypeStruct((SLOTS, 2 * SLOTS), F32),
        compiler_params=params(8),
        cost_estimate=pl.CostEstimate(flops=1 << 18, bytes_accessed=5 << 18, transcendentals=0),
        name="neighbour_sum",
    )(place, same, mine, got)


COMPS = 8 * HALF


def whole(block):
    return block[...].reshape(COMPS, CHUNK)


def hours_of(at, delta):
    return pl.ds(pl.multiple_of(((at + delta) & 7) * CHUNK, CHUNK), CHUNK)


def times(left, right):
    return lax.dot_general(left, right, NT, preferred_element_type=F32)


def early_kernel(place, *refs):
    blocks, (zed, other, mine, theirs, s_1, s_2) = refs[:7], refs[7:]
    core, at = place[0], place[1]

    def add(hours, rows, start):
        wide = rows.astype(F32)
        for out, new in (
            (mine, times(zed[:, hours], rows)),
            (theirs, times(other[:, hours], rows)),
            (s_1, lane_sums(wide)),
            (s_2, lane_sums(wide * wide)),
        ):
            out[...] = new if start else out[...] + new

    @pl.when(core == 0)
    def _():
        for i, (block, delta) in enumerate(zip(blocks, (0, 7, 1, 6, 2, 5, 3))):
            add(hours_of(at, delta), whole(block), i == 0)

    @pl.when(core != 0)
    def _():
        for k in range(NCHUNK):
            rows = jnp.concatenate([block[k] for block in blocks] + [blocks[0][k]], axis=0)
            add(slice(k * CHUNK, (k + 1) * CHUNK), rows, k == 0)


def late_kernel(here, place, far_a, far_b, zed, zsum, acc, *refs):
    core, at = place[0], place[1]
    last = slice(COMPS - HALF, COMPS)
    if here:
        e_1, e_2, out, stats, s_1, s_2 = refs
        s_1[...], s_2[...] = e_1[...], e_2[...]
    else:
        stats, out = refs

    @pl.when(core == 0)
    def _():
        rows = jnp.concatenate([far_a[...], far_b[...]], axis=0).reshape(COMPS, CHUNK)
        out[...] = acc[...] + times(zed[:, hours_of(at, 4)], rows)
        if here:
            wide = rows.astype(F32)
            s_1[...] += lane_sums(wide)
            s_2[...] += lane_sums(wide * wide)

    @pl.when(core != 0)
    def _():
        total = jnp.zeros((SLOTS, 128), F32)
        wide_1 = wide_2 = jnp.zeros((HALF, 128), F32)
        for k in range(NCHUNK):
            rows = far_a[k] if k < 4 else far_b[k - 4]
            total = total + times(zed[:, k * CHUNK : (k + 1) * CHUNK], jnp.concatenate([rows, rows], axis=0))
            if here:
                wide = rows.astype(F32)
                wide_1, wide_2 = wide_1 + lane_sums(wide), wide_2 + lane_sums(wide * wide)
        if here:
            s_1[last], s_2[last] = wide_1, wide_2
        out[:, : COMPS - 128] = acc[:, : COMPS - 128]
        first = lax.broadcasted_iota(jnp.int32, (SLOTS, 128), 1) < HALF
        out[:, COMPS - 128 :] = jnp.where(first, acc[:, COMPS - 128 :], total)

    if here:
        mean = jnp.sum(s_1[...].T, axis=0, keepdims=True) * (1.0 / HOURS)
        square = jnp.sum(s_2[...].T, axis=0, keepdims=True) * (1.0 / HOURS)
        inv = lax.rsqrt(jnp.maximum(square - mean * mean, 0.0) + EPS) * (1.0 / HOURS)
        stats[0:8, :] = jnp.broadcast_to(mean, (8, COMPS))
        stats[8:16, :] = jnp.broadcast_to(inv, (8, COMPS))
    else:
        mean = stats[0:1, :]
        inv = stats[8:9, :]
    out[...] = (out[...] - zsum[:, 0:1] * mean) * inv


def shape(*dims):
    return jax.ShapeDtypeStruct(dims, F32)


def make_early(place, blocks, zed, other):
    return pl.pallas_call(
        early_kernel,
        in_specs=[SMEM] + [VMEM] * 9,
        out_specs=[VMEM] * 4,
        out_shape=[shape(SLOTS, COMPS)] * 2 + [shape(COMPS, 128)] * 2,
        compiler_params=params(24),
        cost_estimate=pl.CostEstimate(flops=15 << 27, bytes_accessed=9 << 20, transcendentals=0),
        name="early_composites",
    )(place, *blocks, zed, other)


def make_late(place, blocks, zed, zsum, acc, sums=None, stats=None):
    here = stats is None
    scratch = [pltpu.VMEM((COMPS, 128), F32)] * 2 if here else []
    extra = list(sums) if here else [stats]
    return pl.pallas_call(
        functools.partial(late_kernel, here),
        in_specs=[SMEM] + [VMEM] * (5 + len(extra)),
        out_specs=[VMEM] * (2 if here else 1),
        out_shape=[shape(SLOTS, COMPS)] + ([shape(16, COMPS)] if here else []),
        scratch_shapes=scratch,
        compiler_params=params(24),
        cost_estimate=pl.CostEstimate(flops=1 << 27, bytes_accessed=4 << 20, transcendentals=0),
        name="late_composites",
    )(place, *blocks, zed, zsum, acc, *extra)


def merge_kernel(place, mine, got, out):
    core, z, step = place[0], place[2], pl.program_id(0)
    first = lax.broadcasted_iota(jnp.int32, (SLOTS, 128), 1) < HALF
    tile = pl.ds(pl.multiple_of(step * 128, 128), 128)
    low = jnp.where(core == 0, mine[:, tile], got[:, tile])
    for odd in range(2):
        d = (2 * step + odd - z) & 7
        slot = jnp.where(d == 0, 0, jnp.where(d == 4, 7, jnp.where(d < 4, 2 * d, 15 - 2 * d)))
        tile = pl.ds(pl.multiple_of((slot >> 1) * 128, 128), 128)
        rows = jnp.where(core == 0, got[:, tile], mine[:, tile])
        high = jnp.where((slot & 1) == 1, rows, pltpu.roll(rows, HALF, 1))
        out[:, odd * 128 : odd * 128 + 128] = jnp.where(first, pltpu.roll(low, HALF, 1) if odd else low, high)


def merge(place, mine, got):
    return pl.pallas_call(
        merge_kernel,
        grid=(4,),
        in_specs=[SMEM, VMEM, VMEM],
        out_specs=pl.BlockSpec((SLOTS, 256), lambda i: (0, i)),
        out_shape=shape(SLOTS, 1024),
        compiler_params=params(8),
        cost_estimate=pl.CostEstimate(flops=1 << 20, bytes_accessed=2 << 20, transcendentals=0),
        name="merge_halves",
    )(place, mine, got)


def groups_and_rings():
    number = lambda z, y, x, c: ((z * 8 + y) * 4 + x) * 2 + c
    line = [(i, x) for i in range(8) for x in range(4)]
    groups = [[number(z, y, x, 0) for z, x in line] for y in range(8)]
    groups += [[number(z, y, x, 1) for y, x in line] for z in range(8)]
    up = []
    for z in range(8):
        for y in range(8):
            for x in range(4):
                up.append((number(z, y, x, 0), number(z, (y + 1) % 8, x, 0)))
                up.append((number(z, y, x, 1), number((z + 1) % 8, y, x, 1)))
    return groups, up, [(j, i) for i, j in up]


def per_device(anomalies, station_count, composite_of):
    core, y, z = (lax.axis_index(name).astype(jnp.int32) for name in ("c", "y", "z"))
    place = jnp.stack([core, jnp.where(core == 0, y, z), z])
    swap = [(0, 1), (1, 0)]
    every = ("z", "y", "x", "c")
    together = lax.optimization_barrier
    groups, up, down = groups_and_rings()
    zed, edge, own, theirs = make_zed(station_count, place, composite_of.reshape(1, SLOTS), anomalies)

    got = lax.ppermute(theirs, "c", swap)
    part = (own + got.astype(F32)).astype(BF16).reshape(32, 16, CHUNK)
    part, zed, edge = together((part, zed, edge))
    blocks = lax.all_to_all(part, ("y", "x"), split_axis=0, concat_axis=0, tiled=True)
    block = jnp.sum(blocks.astype(F32), axis=0).astype(BF16)

    across = [(i, i + 1) for i in range(1, 63, 2)]
    across += [(j, i) for i, j in across]
    other = lax.ppermute(zed, "c", swap)
    halo = lax.ppermute(edge, every[1:], across)
    same, near_mine, near_theirs, zsum, osum = make_near(place, zed, other, halo)
    near_got = lax.ppermute(near_theirs, every[1:], across)

    spread = jnp.broadcast_to(block, (32, 16, CHUNK))
    first = lax.all_to_all(spread, every, split_axis=0, concat_axis=0, axis_index_groups=groups, tiled=True)
    first, near_got = together((first.reshape(8, HALF, CHUNK), near_got))
    before, after = [first], [first]
    for step in range(3):
        before.append(lax.ppermute(before[step], every, up))
        after.append(lax.ppermute(after[step], every, down))
    far = [lax.ppermute(before[3][:4], every, up), lax.ppermute(after[3][4:], every, down)]

    near_corr = near_sum(place, same, near_mine, near_got)
    near_blocks = [first, before[1], after[1], before[2], after[2], before[3], after[3]]
    early = make_early(place, near_blocks, zed, other)
    far[0], near_corr = together((far[0], near_corr))
    for_other, stats = make_late(place, far, other, osum, early[1], sums=early[2:])
    back = lax.ppermute(for_other, "c", swap)
    (mine,) = make_late(place, far, zed, zsum, early[0], stats=stats)
    return near_corr, merge(place, mine, back)


def solution(mesh):
    grid = Mesh(mesh.devices.reshape(8, 8, 4, 2), ("z", "y", "x", "c"))
    axes = ("z", "y", "x", "c")
    return jax.shard_map(
        per_device,
        mesh=grid,
        in_specs=(P(axes, None), P(axes), P(axes)),
        out_specs=(P(axes, None), P(axes, None)),
        check_vma=False,
    )
```

```python
import functools

import jax
import jax.numpy as jnp
from jax import lax
from jax.experimental import pallas as pl
from jax.experimental.pallas import tpu as pltpu
from jax.sharding import Mesh, PartitionSpec as P

HOURS = 4096
SLOTS = 256
COMP_REG = 128
HALF = COMP_REG // 2
EPS = 1e-05
CHUNK = 512
NCHUNK = HOURS // CHUNK
ROWS = 32
MERGE = 64
F32 = jnp.float32
BF16 = jnp.bfloat16
SMEM = pl.BlockSpec(memory_space=pltpu.SMEM)
NT = (((1,), (1,)), ((), ()))


def params(mib):
    return pltpu.CompilerParams(vmem_limit_bytes=mib << 20)


VMEM = pl.BlockSpec(memory_space=pltpu.VMEM)
HBM = pl.BlockSpec(memory_space=pltpu.HBM)


def zed_kernel(count, core, ids, x, zed, edge, own, theirs, held, sems):
    steps = SLOTS // ROWS
    rows_of = lambda step: pl.ds(step * ROWS, ROWS)
    copies = [
        pltpu.make_async_copy(x.at[rows_of(step)], held.at[rows_of(step)], sems.at[step]) for step in range(steps)
    ]
    for copy in copies:
        copy.start()
    for step, copy in enumerate(copies):
        copy.wait()
        values = held[rows_of(step), :].astype(F32)
        center = values - jnp.mean(values, axis=1, keepdims=True)
        scale = lax.rsqrt(jnp.mean(center * center, axis=1, keepdims=True) + EPS)
        slot = step * ROWS + lax.broadcasted_iota(jnp.int32, (ROWS, 1), 0)
        live = (slot < count[0]).astype(F32)
        rows = (center * scale * live).astype(BF16)
        zed[rows_of(step), :] = rows
        edge[rows_of(step), :] = jnp.where(core[0] == 0, rows[:, : HOURS // 2], rows[:, HOURS // 2 :])

    index = lax.broadcasted_iota(jnp.int32, (COMP_REG, SLOTS), 0)
    index = (index + HALF * core[0]) & (COMP_REG - 1)
    hot = (ids[...] == index).astype(F32).astype(BF16)
    for k in range(NCHUNK):
        part = jnp.dot(hot, zed[:, k * CHUNK : (k + 1) * CHUNK], preferred_element_type=F32)
        own[k] = part[:HALF]
        theirs[k] = part[HALF:].astype(BF16)


def make_zed(count, core, ids, x):
    block = (NCHUNK, HALF, CHUNK)
    return pl.pallas_call(
        zed_kernel,
        in_specs=[SMEM, SMEM, VMEM, HBM],
        out_specs=[VMEM] * 4,
        out_shape=[
            jax.ShapeDtypeStruct((SLOTS, HOURS), BF16),
            jax.ShapeDtypeStruct((SLOTS, HOURS // 2), BF16),
            jax.ShapeDtypeStruct(block, F32),
            jax.ShapeDtypeStruct(block, BF16),
        ],
        scratch_shapes=[pltpu.VMEM((SLOTS, HOURS), BF16), pltpu.SemaphoreType.DMA((SLOTS // ROWS,))],
        compiler_params=params(48),
        cost_estimate=pl.CostEstimate(flops=300_000_000, bytes_accessed=6 << 20, transcendentals=0),
        name="normalize_and_sum",
    )(count, core, ids, x)


def lane_sums(block):
    wide = block[:, :128]
    for k in range(1, block.shape[1] // 128):
        wide = wide + block[:, k * 128 : (k + 1) * 128]
    return wide


def row_sums(rows, out):
    wide = lane_sums(rows[:, :CHUNK].astype(F32))
    for k in range(1, NCHUNK):
        wide = wide + lane_sums(rows[:, k * CHUNK : (k + 1) * CHUNK].astype(F32))
    out[...] = jnp.broadcast_to(jnp.sum(wide, axis=1, keepdims=True), out.shape)


def edge_kernel(core, zed, halo, mine, theirs, zsum):
    def products(half):
        mine[...] = times(half, halo[...])
        theirs[...] = times(halo[...], half).astype(BF16)

    pl.when(core[0] == 0)(lambda: products(zed[:, HOURS // 2 :]))
    pl.when(core[0] != 0)(lambda: products(zed[:, : HOURS // 2]))
    row_sums(zed, zsum)


def make_edge(place, zed, halo):
    return pl.pallas_call(
        edge_kernel,
        in_specs=[SMEM, VMEM, VMEM],
        out_specs=[VMEM] * 3,
        out_shape=[shape(SLOTS, SLOTS), jax.ShapeDtypeStruct((SLOTS, SLOTS), BF16), shape(SLOTS, 128)],
        compiler_params=params(16),
        cost_estimate=pl.CostEstimate(flops=1 << 29, bytes_accessed=4 << 20, transcendentals=0),
        name="edge_products",
    )(place, zed, halo)


def near_kernel(core, zed, other, mine, got, near, osum, held):
    at = pl.multiple_of(core[0] * SLOTS, SLOTS)
    near[:, pl.ds(at, SLOTS)] = (mine[...] + got[...].astype(F32)) * (1.0 / HOURS)
    near[:, pl.ds(SLOTS - at, SLOTS)] = times(zed[...], other[...]) * (1.0 / HOURS)
    row_sums(other, osum)
    held[...] = other[...]


def make_near(place, zed, other, mine, got):
    return pl.pallas_call(
        near_kernel,
        in_specs=[SMEM] + [VMEM] * 4,
        out_specs=[VMEM] * 3,
        out_shape=[
            shape(SLOTS, 2 * SLOTS),
            shape(SLOTS, 128),
            jax.ShapeDtypeStruct((SLOTS, HOURS), BF16),
        ],
        compiler_params=params(16),
        cost_estimate=pl.CostEstimate(flops=1 << 29, bytes_accessed=5 << 20, transcendentals=0),
        name="neighbour_correlation",
    )(place, zed, other, mine, got)


COMPS = 8 * HALF


def whole(block):
    return block[...].reshape(COMPS, CHUNK)


def hours_of(at, delta):
    return pl.ds(pl.multiple_of(((at + delta) & 7) * CHUNK, CHUNK), CHUNK)


def times(left, right):
    return lax.dot_general(left, right, NT, preferred_element_type=F32)


def early_kernel(place, *refs):
    blocks, (zed, other, mine, theirs, s_1, s_2) = refs[:7], refs[7:]
    core, at = place[0], place[1]

    def add(hours, rows, start):
        wide = rows.astype(F32)
        for out, new in (
            (mine, times(zed[:, hours], rows)),
            (theirs, times(other[:, hours], rows)),
            (s_1, lane_sums(wide)),
            (s_2, lane_sums(wide * wide)),
        ):
            out[...] = new if start else out[...] + new

    @pl.when(core == 0)
    def _():
        for i, (block, delta) in enumerate(zip(blocks, (0, 7, 1, 6, 2, 5, 3))):
            add(hours_of(at, delta), whole(block), i == 0)

    @pl.when(core != 0)
    def _():
        for k in range(NCHUNK):
            rows = jnp.concatenate([block[k] for block in blocks] + [blocks[0][k]], axis=0)
            add(slice(k * CHUNK, (k + 1) * CHUNK), rows, k == 0)


def late_kernel(here, place, far, zed, zsum, acc, *refs):
    core, at = place[0], place[1]
    last = slice(COMPS - HALF, COMPS)
    if here:
        e_1, e_2, out, stats, s_1, s_2 = refs
        s_1[...], s_2[...] = e_1[...], e_2[...]
    else:
        stats, out = refs

    @pl.when(core == 0)
    def _():
        rows = whole(far)
        out[...] = acc[...] + times(zed[:, hours_of(at, 4)], rows)
        if here:
            wide = rows.astype(F32)
            s_1[...] += lane_sums(wide)
            s_2[...] += lane_sums(wide * wide)

    @pl.when(core != 0)
    def _():
        total = jnp.zeros((SLOTS, 128), F32)
        wide_1 = wide_2 = jnp.zeros((HALF, 128), F32)
        for k in range(NCHUNK):
            rows = far[k]
            total = total + times(zed[:, k * CHUNK : (k + 1) * CHUNK], jnp.concatenate([rows, rows], axis=0))
            if here:
                wide = rows.astype(F32)
                wide_1, wide_2 = wide_1 + lane_sums(wide), wide_2 + lane_sums(wide * wide)
        if here:
            s_1[last], s_2[last] = wide_1, wide_2
        out[:, : COMPS - 128] = acc[:, : COMPS - 128]
        first = lax.broadcasted_iota(jnp.int32, (SLOTS, 128), 1) < HALF
        out[:, COMPS - 128 :] = jnp.where(first, acc[:, COMPS - 128 :], total)

    if here:
        mean = jnp.sum(s_1[...].T, axis=0, keepdims=True) * (1.0 / HOURS)
        square = jnp.sum(s_2[...].T, axis=0, keepdims=True) * (1.0 / HOURS)
        inv = lax.rsqrt(jnp.maximum(square - mean * mean, 0.0) + EPS) * (1.0 / HOURS)
        stats[0:8, :] = jnp.broadcast_to(mean, (8, COMPS))
        stats[8:16, :] = jnp.broadcast_to(inv, (8, COMPS))
    else:
        mean = stats[0:1, :]
        inv = stats[8:9, :]
    out[...] = (out[...] - zsum[:, 0:1] * mean) * inv


def shape(*dims):
    return jax.ShapeDtypeStruct(dims, F32)


def make_early(place, blocks, zed, other):
    return pl.pallas_call(
        early_kernel,
        in_specs=[SMEM] + [VMEM] * 9,
        out_specs=[VMEM] * 4,
        out_shape=[shape(SLOTS, COMPS)] * 2 + [shape(COMPS, 128)] * 2,
        compiler_params=params(24),
        cost_estimate=pl.CostEstimate(flops=15 << 27, bytes_accessed=9 << 20, transcendentals=0),
        name="early_composites",
    )(place, *blocks, zed, other)


def make_late(place, far, zed, zsum, acc, sums=None, stats=None):
    here = stats is None
    scratch = [pltpu.VMEM((COMPS, 128), F32)] * 2 if here else []
    extra = list(sums) if here else [stats]
    return pl.pallas_call(
        functools.partial(late_kernel, here),
        in_specs=[SMEM] + [VMEM] * (4 + len(extra)),
        out_specs=[VMEM] * (2 if here else 1),
        out_shape=[shape(SLOTS, COMPS)] + ([shape(16, COMPS)] if here else []),
        scratch_shapes=scratch,
        compiler_params=params(24),
        cost_estimate=pl.CostEstimate(flops=1 << 27, bytes_accessed=4 << 20, transcendentals=0),
        name="late_composites",
    )(place, far, zed, zsum, acc, *extra)


def merge_kernel(place, mine, got, out, held, sems):
    core, z = place[0], place[2]
    first = lax.broadcasted_iota(jnp.int32, (MERGE, 128), 1) < HALF
    copies = []
    for r in range(SLOTS // MERGE):
        rows = slice(r * MERGE, (r + 1) * MERGE)
        for to in range(8):
            tile = slice(to // 2 * 128, to // 2 * 128 + 128)
            low = jnp.where(core == 0, mine[rows, tile], got[rows, tile])
            d = (to - z) & 7
            slot = jnp.where(d == 0, 0, jnp.where(d == 4, 7, jnp.where(d < 4, 2 * d, 15 - 2 * d)))
            tile = pl.ds(pl.multiple_of((slot >> 1) * 128, 128), 128)
            high = jnp.where(core == 0, got[rows, tile], mine[rows, tile])
            high = jnp.where((slot & 1) == 1, high, pltpu.roll(high, HALF, 1))
            low = pltpu.roll(low, HALF, 1) if to % 2 else low
            held[rows, to * 128 : to * 128 + 128] = jnp.where(first, low, high)
        copies.append(pltpu.make_async_copy(held.at[rows], out.at[rows], sems.at[r]))
        copies[-1].start()
    for copy in copies:
        copy.wait()


def merge(place, mine, got):
    return pl.pallas_call(
        merge_kernel,
        in_specs=[SMEM, VMEM, VMEM],
        out_specs=pl.BlockSpec(memory_space=pl.ANY),
        out_shape=shape(SLOTS, 1024),
        scratch_shapes=[pltpu.VMEM((SLOTS, 1024), F32), pltpu.SemaphoreType.DMA((SLOTS // MERGE,))],
        compiler_params=params(8),
        cost_estimate=pl.CostEstimate(flops=1 << 20, bytes_accessed=2 << 20, transcendentals=0),
        name="merge_halves",
    )(place, mine, got)


def spread_kernel(blocks, out):
    total = blocks[0].astype(F32)
    for i in range(1, 32):
        total = total + blocks[i].astype(F32)
    rows = total.astype(BF16)
    for i in range(32):
        out[i] = rows


def sum_and_spread(blocks):
    return pl.pallas_call(
        spread_kernel,
        in_specs=[VMEM],
        out_specs=VMEM,
        out_shape=jax.ShapeDtypeStruct(blocks.shape, BF16),
        compiler_params=params(8),
        cost_estimate=pl.CostEstimate(flops=1 << 18, bytes_accessed=1 << 20, transcendentals=0),
        name="sum_and_spread",
    )(blocks)


def groups_and_rings():
    number = lambda z, y, x, c: ((z * 8 + y) * 4 + x) * 2 + c
    line = [(i, x) for i in range(8) for x in range(4)]
    groups = [[number(z, y, x, 0) for z, x in line] for y in range(8)]
    groups += [[number(z, y, x, 1) for y, x in line] for z in range(8)]
    up = []
    for z in range(8):
        for y in range(8):
            for x in range(4):
                up.append((number(z, y, x, 0), number(z, (y + 1) % 8, x, 0)))
                up.append((number(z, y, x, 1), number((z + 1) % 8, y, x, 1)))
    return groups, up, [(j, i) for i, j in up]


def per_device(anomalies, station_count, composite_of):
    core, y, z = (lax.axis_index(name).astype(jnp.int32) for name in ("c", "y", "z"))
    place = jnp.stack([core, jnp.where(core == 0, y, z), z])
    swap = [(0, 1), (1, 0)]
    every = ("z", "y", "x", "c")
    together = lax.optimization_barrier
    groups, up, down = groups_and_rings()
    zed, edge, own, theirs = make_zed(station_count, place, composite_of.reshape(1, SLOTS), anomalies)

    got = lax.ppermute(theirs, "c", swap)
    part = (own + got.astype(F32)).astype(BF16).reshape(32, 16, CHUNK)
    part, edge = together((part, edge))
    across = [(i, i + 1) for i in range(1, 63, 2)]
    across += [(j, i) for i, j in across]
    halo = lax.ppermute(edge, every[1:], across)
    blocks = lax.all_to_all(part, ("y", "x"), split_axis=0, concat_axis=0, tiled=True)
    spread = sum_and_spread(blocks)

    near_mine, near_theirs, zsum = make_edge(place, zed, halo)
    near_theirs, zed = together((near_theirs, zed))
    near_got = lax.ppermute(near_theirs, every[1:], across)
    other = lax.ppermute(zed, "c", swap)
    first = lax.all_to_all(spread, every, split_axis=0, concat_axis=0, axis_index_groups=groups, tiled=True)
    first, near_got = together((first.reshape(8, HALF, CHUNK), near_got))

    above, below = [first], [first]
    for step in range(3):
        if step == 2:
            near_corr, osum, other = make_near(place, zed, other, near_mine, near_got)
            below[2], near_corr = together((below[2], near_corr))
        above.append(lax.ppermute(above[step], every, up))
        below.append(lax.ppermute(below[step], every, down))
    far = lax.ppermute(above[3], every, up)

    blocks = [first, above[1], below[1], above[2], below[2], above[3], below[3]]
    early = make_early(place, blocks, zed, other)
    for_other, stats = make_late(place, far, other, osum, early[1], sums=early[2:])
    back = lax.ppermute(for_other, "c", swap)
    (mine,) = make_late(place, far, zed, zsum, early[0], stats=stats)
    return near_corr, merge(place, mine, back)


def solution(mesh):
    grid = Mesh(mesh.devices.reshape(8, 8, 4, 2), ("z", "y", "x", "c"))
    axes = ("z", "y", "x", "c")
    return jax.shard_map(
        per_device,
        mesh=grid,
        in_specs=(P(axes, None), P(axes), P(axes)),
        out_specs=(P(axes, None), P(axes, None)),
        check_vma=False,
    )
```

```python
import functools

import jax
import jax.numpy as jnp
from jax import lax
from jax.experimental import pallas as pl
from jax.experimental.pallas import tpu as pltpu
from jax.sharding import Mesh, PartitionSpec as P

HOURS = 4096
SLOTS = 256
COMP_REG = 128
HALF = COMP_REG // 2
EPS = 1e-05
CHUNK = 512
NCHUNK = HOURS // CHUNK
ROWS = 32
MERGE = 64
F32 = jnp.float32
BF16 = jnp.bfloat16
SMEM = pl.BlockSpec(memory_space=pltpu.SMEM)
NT = (((1,), (1,)), ((), ()))


def params(mib):
    return pltpu.CompilerParams(vmem_limit_bytes=mib << 20)


VMEM = pl.BlockSpec(memory_space=pltpu.VMEM)
HBM = pl.BlockSpec(memory_space=pltpu.HBM)


def sum_of(pieces):
    sums = pieces[:4]
    for i, piece in enumerate(pieces[4:]):
        sums[i % 4] = sums[i % 4] + piece
    return (sums[0] + sums[1]) + (sums[2] + sums[3])


def zed_kernel(count, core, ids, x, zed, edge, own, theirs, held, sems):
    steps = SLOTS // ROWS
    rows_of = lambda step: pl.ds(step * ROWS, ROWS)
    copies = [
        pltpu.make_async_copy(x.at[rows_of(step)], held.at[rows_of(step)], sems.at[step]) for step in range(steps)
    ]
    for copy in copies:
        copy.start()
    for step, copy in enumerate(copies):
        copy.wait()
        pieces = [held[rows_of(step), k * 128 : k * 128 + 128].astype(F32) for k in range(HOURS // 128)]
        mean = jnp.sum(sum_of(pieces), axis=1, keepdims=True) * (1.0 / HOURS)
        squares = sum_of([jnp.square(piece - mean) for piece in pieces])
        scale = lax.rsqrt(jnp.sum(squares, axis=1, keepdims=True) * (1.0 / HOURS) + EPS)
        slot = step * ROWS + lax.broadcasted_iota(jnp.int32, (ROWS, 1), 0)
        scale = scale * (slot < count[0]).astype(F32)
        for k in range(HOURS // 256):
            early, late = (((pieces[i] - mean) * scale).astype(BF16) for i in (k, k + HOURS // 256))
            zed[rows_of(step), k * 128 : k * 128 + 128] = early
            zed[rows_of(step), HOURS // 2 + k * 128 : HOURS // 2 + k * 128 + 128] = late
            edge[rows_of(step), k * 128 : k * 128 + 128] = jnp.where(core[0] == 0, early, late)

    index = lax.broadcasted_iota(jnp.int32, (COMP_REG, SLOTS), 0)
    index = (index + HALF * core[0]) & (COMP_REG - 1)
    hot = (ids[...] == index).astype(F32).astype(BF16)
    for k in range(NCHUNK):
        part = jnp.dot(hot, zed[:, k * CHUNK : (k + 1) * CHUNK], preferred_element_type=F32)
        own[k] = part[:HALF]
        theirs[k] = part[HALF:].astype(BF16)


def make_zed(count, core, ids, x):
    block = (NCHUNK, HALF, CHUNK)
    return pl.pallas_call(
        zed_kernel,
        in_specs=[SMEM, SMEM, VMEM, HBM],
        out_specs=[VMEM] * 4,
        out_shape=[
            jax.ShapeDtypeStruct((SLOTS, HOURS), BF16),
            jax.ShapeDtypeStruct((SLOTS, HOURS // 2), BF16),
            jax.ShapeDtypeStruct(block, F32),
            jax.ShapeDtypeStruct(block, BF16),
        ],
        scratch_shapes=[pltpu.VMEM((SLOTS, HOURS), BF16), pltpu.SemaphoreType.DMA((SLOTS // ROWS,))],
        compiler_params=params(48),
        cost_estimate=pl.CostEstimate(flops=300_000_000, bytes_accessed=6 << 20, transcendentals=0),
        name="normalize_and_sum",
    )(count, core, ids, x)


def lane_sums(block):
    wide = block[:, :128]
    for k in range(1, block.shape[1] // 128):
        wide = wide + block[:, k * 128 : (k + 1) * 128]
    return wide


def row_sums(rows, out):
    wide = lane_sums(rows[:, :CHUNK].astype(F32))
    for k in range(1, NCHUNK):
        wide = wide + lane_sums(rows[:, k * CHUNK : (k + 1) * CHUNK].astype(F32))
    out[...] = jnp.broadcast_to(jnp.sum(wide, axis=1, keepdims=True), out.shape)


def edge_kernel(core, zed, halo, mine, theirs, zsum):
    def products(half):
        mine[...] = times(half, halo[...])
        theirs[...] = times(halo[...], half).astype(BF16)

    pl.when(core[0] == 0)(lambda: products(zed[:, HOURS // 2 :]))
    pl.when(core[0] != 0)(lambda: products(zed[:, : HOURS // 2]))
    row_sums(zed, zsum)


def make_edge(place, zed, halo):
    return pl.pallas_call(
        edge_kernel,
        in_specs=[SMEM, VMEM, VMEM],
        out_specs=[VMEM] * 3,
        out_shape=[shape(SLOTS, SLOTS), jax.ShapeDtypeStruct((SLOTS, SLOTS), BF16), shape(SLOTS, 128)],
        compiler_params=params(16),
        cost_estimate=pl.CostEstimate(flops=1 << 29, bytes_accessed=4 << 20, transcendentals=0),
        name="edge_products",
    )(place, zed, halo)


def near_kernel(core, zed, other, mine, got, near, osum, held):
    at = pl.multiple_of(core[0] * SLOTS, SLOTS)
    near[:, pl.ds(at, SLOTS)] = (mine[...] + got[...].astype(F32)) * (1.0 / HOURS)
    near[:, pl.ds(SLOTS - at, SLOTS)] = times(zed[...], other[...]) * (1.0 / HOURS)
    row_sums(other, osum)
    held[...] = other[...]


def make_near(place, zed, other, mine, got):
    return pl.pallas_call(
        near_kernel,
        in_specs=[SMEM] + [VMEM] * 4,
        out_specs=[VMEM] * 3,
        out_shape=[
            shape(SLOTS, 2 * SLOTS),
            shape(SLOTS, 128),
            jax.ShapeDtypeStruct((SLOTS, HOURS), BF16),
        ],
        compiler_params=params(16),
        cost_estimate=pl.CostEstimate(flops=1 << 29, bytes_accessed=5 << 20, transcendentals=0),
        name="neighbour_correlation",
    )(place, zed, other, mine, got)


COMPS = 8 * HALF


def whole(block):
    return block[...].reshape(COMPS, CHUNK)


def hours_of(at, delta):
    return pl.ds(pl.multiple_of(((at + delta) & 7) * CHUNK, CHUNK), CHUNK)


def times(left, right):
    return lax.dot_general(left, right, NT, preferred_element_type=F32)


def early_kernel(place, *refs):
    blocks, (zed, other, mine, theirs, s_1, s_2) = refs[:7], refs[7:]
    core, at = place[0], place[1]

    def add(hours, rows, start):
        wide = rows.astype(F32)
        for out, new in (
            (mine, times(zed[:, hours], rows)),
            (theirs, times(other[:, hours], rows)),
            (s_1, lane_sums(wide)),
            (s_2, lane_sums(wide * wide)),
        ):
            out[...] = new if start else out[...] + new

    @pl.when(core == 0)
    def _():
        for i, (block, delta) in enumerate(zip(blocks, (0, 7, 1, 6, 2, 5, 3))):
            add(hours_of(at, delta), whole(block), i == 0)

    @pl.when(core != 0)
    def _():
        for k in range(NCHUNK):
            rows = jnp.concatenate([block[k] for block in blocks] + [blocks[0][k]], axis=0)
            add(slice(k * CHUNK, (k + 1) * CHUNK), rows, k == 0)


def late_kernel(here, place, far, zed, zsum, acc, *refs):
    core, at = place[0], place[1]
    last = slice(COMPS - HALF, COMPS)
    if here:
        e_1, e_2, out, stats, s_1, s_2 = refs
        s_1[...], s_2[...] = e_1[...], e_2[...]
    else:
        stats, out = refs

    @pl.when(core == 0)
    def _():
        rows = whole(far)
        out[...] = acc[...] + times(zed[:, hours_of(at, 4)], rows)
        if here:
            wide = rows.astype(F32)
            s_1[...] += lane_sums(wide)
            s_2[...] += lane_sums(wide * wide)

    @pl.when(core != 0)
    def _():
        total = jnp.zeros((SLOTS, 128), F32)
        wide_1 = wide_2 = jnp.zeros((HALF, 128), F32)
        for k in range(NCHUNK):
            rows = far[k]
            total = total + times(zed[:, k * CHUNK : (k + 1) * CHUNK], jnp.concatenate([rows, rows], axis=0))
            if here:
                wide = rows.astype(F32)
                wide_1, wide_2 = wide_1 + lane_sums(wide), wide_2 + lane_sums(wide * wide)
        if here:
            s_1[last], s_2[last] = wide_1, wide_2
        out[:, : COMPS - 128] = acc[:, : COMPS - 128]
        first = lax.broadcasted_iota(jnp.int32, (SLOTS, 128), 1) < HALF
        out[:, COMPS - 128 :] = jnp.where(first, acc[:, COMPS - 128 :], total)

    if here:
        mean = jnp.sum(s_1[...].T, axis=0, keepdims=True) * (1.0 / HOURS)
        square = jnp.sum(s_2[...].T, axis=0, keepdims=True) * (1.0 / HOURS)
        inv = lax.rsqrt(jnp.maximum(square - mean * mean, 0.0) + EPS) * (1.0 / HOURS)
        stats[0:8, :] = jnp.broadcast_to(mean, (8, COMPS))
        stats[8:16, :] = jnp.broadcast_to(inv, (8, COMPS))
    else:
        mean = stats[0:1, :]
        inv = stats[8:9, :]
    out[...] = (out[...] - zsum[:, 0:1] * mean) * inv


def shape(*dims):
    return jax.ShapeDtypeStruct(dims, F32)


def make_early(place, blocks, zed, other):
    return pl.pallas_call(
        early_kernel,
        in_specs=[SMEM] + [VMEM] * 9,
        out_specs=[VMEM] * 4,
        out_shape=[shape(SLOTS, COMPS)] * 2 + [shape(COMPS, 128)] * 2,
        compiler_params=params(24),
        cost_estimate=pl.CostEstimate(flops=15 << 27, bytes_accessed=9 << 20, transcendentals=0),
        name="early_composites",
    )(place, *blocks, zed, other)


def make_late(place, far, zed, zsum, acc, sums=None, stats=None):
    here = stats is None
    scratch = [pltpu.VMEM((COMPS, 128), F32)] * 2 if here else []
    extra = list(sums) if here else [stats]
    return pl.pallas_call(
        functools.partial(late_kernel, here),
        in_specs=[SMEM] + [VMEM] * (4 + len(extra)),
        out_specs=[VMEM] * (2 if here else 1),
        out_shape=[shape(SLOTS, COMPS)] + ([shape(16, COMPS)] if here else []),
        scratch_shapes=scratch,
        compiler_params=params(24),
        cost_estimate=pl.CostEstimate(flops=1 << 27, bytes_accessed=4 << 20, transcendentals=0),
        name="late_composites",
    )(place, far, zed, zsum, acc, *extra)


def merge_kernel(place, mine, got, out, held, sems):
    core, z = place[0], place[2]
    first = lax.broadcasted_iota(jnp.int32, (MERGE, 128), 1) < HALF
    copies = []
    for r in range(SLOTS // MERGE):
        rows = slice(r * MERGE, (r + 1) * MERGE)
        for to in range(8):
            tile = slice(to // 2 * 128, to // 2 * 128 + 128)
            low = jnp.where(core == 0, mine[rows, tile], got[rows, tile])
            d = (to - z) & 7
            slot = jnp.where(d == 0, 0, jnp.where(d == 4, 7, jnp.where(d < 4, 2 * d, 15 - 2 * d)))
            tile = pl.ds(pl.multiple_of((slot >> 1) * 128, 128), 128)
            high = jnp.where(core == 0, got[rows, tile], mine[rows, tile])
            high = jnp.where((slot & 1) == 1, high, pltpu.roll(high, HALF, 1))
            low = pltpu.roll(low, HALF, 1) if to % 2 else low
            held[rows, to * 128 : to * 128 + 128] = jnp.where(first, low, high)
        copies.append(pltpu.make_async_copy(held.at[rows], out.at[rows], sems.at[r]))
        copies[-1].start()
    for copy in copies:
        copy.wait()


def merge(place, mine, got):
    return pl.pallas_call(
        merge_kernel,
        in_specs=[SMEM, VMEM, VMEM],
        out_specs=pl.BlockSpec(memory_space=pl.ANY),
        out_shape=shape(SLOTS, 1024),
        scratch_shapes=[pltpu.VMEM((SLOTS, 1024), F32), pltpu.SemaphoreType.DMA((SLOTS // MERGE,))],
        compiler_params=params(8),
        cost_estimate=pl.CostEstimate(flops=1 << 20, bytes_accessed=2 << 20, transcendentals=0),
        name="merge_halves",
    )(place, mine, got)


def spread_kernel(blocks, out):
    total = blocks[0].astype(F32)
    for i in range(1, 32):
        total = total + blocks[i].astype(F32)
    rows = total.astype(BF16)
    for i in range(32):
        out[i] = rows


def sum_and_spread(blocks):
    return pl.pallas_call(
        spread_kernel,
        in_specs=[VMEM],
        out_specs=VMEM,
        out_shape=jax.ShapeDtypeStruct(blocks.shape, BF16),
        compiler_params=params(8),
        cost_estimate=pl.CostEstimate(flops=1 << 18, bytes_accessed=1 << 20, transcendentals=0),
        name="sum_and_spread",
    )(blocks)


def groups_and_rings():
    number = lambda z, y, x, c: ((z * 8 + y) * 4 + x) * 2 + c
    line = [(i, x) for i in range(8) for x in range(4)]
    groups = [[number(z, y, x, 0) for z, x in line] for y in range(8)]
    groups += [[number(z, y, x, 1) for y, x in line] for z in range(8)]
    up = []
    for z in range(8):
        for y in range(8):
            for x in range(4):
                up.append((number(z, y, x, 0), number(z, (y + 1) % 8, x, 0)))
                up.append((number(z, y, x, 1), number((z + 1) % 8, y, x, 1)))
    return groups, up, [(j, i) for i, j in up]


def per_device(anomalies, station_count, composite_of):
    core, y, z = (lax.axis_index(name).astype(jnp.int32) for name in ("c", "y", "z"))
    place = jnp.stack([core, jnp.where(core == 0, y, z), z])
    swap = [(0, 1), (1, 0)]
    every = ("z", "y", "x", "c")
    together = lax.optimization_barrier
    groups, up, down = groups_and_rings()
    zed, edge, own, theirs = make_zed(station_count, place, composite_of.reshape(1, SLOTS), anomalies)

    got = lax.ppermute(theirs, "c", swap)
    part = (own + got.astype(F32)).astype(BF16).reshape(32, 16, CHUNK)
    part, edge = together((part, edge))
    across = [(i, i + 1) for i in range(1, 63, 2)]
    across += [(j, i) for i, j in across]
    halo = lax.ppermute(edge, every[1:], across)
    blocks = lax.all_to_all(part, ("y", "x"), split_axis=0, concat_axis=0, tiled=True)
    spread = sum_and_spread(blocks)

    near_mine, near_theirs, zsum = make_edge(place, zed, halo)
    near_theirs, zed = together((near_theirs, zed))
    near_got = lax.ppermute(near_theirs, every[1:], across)
    other = lax.ppermute(zed, "c", swap)
    first = lax.all_to_all(spread, every, split_axis=0, concat_axis=0, axis_index_groups=groups, tiled=True)
    first, near_got = together((first.reshape(8, HALF, CHUNK), near_got))

    above, below = [first], [first]
    for step in range(3):
        if step == 2:
            near_corr, osum, other = make_near(place, zed, other, near_mine, near_got)
            below[2], near_corr = together((below[2], near_corr))
        above.append(lax.ppermute(above[step], every, up))
        below.append(lax.ppermute(below[step], every, down))
    far = lax.ppermute(above[3], every, up)

    blocks = [first, above[1], below[1], above[2], below[2], above[3], below[3]]
    early = make_early(place, blocks, zed, other)
    for_other, stats = make_late(place, far, other, osum, early[1], sums=early[2:])
    back = lax.ppermute(for_other, "c", swap)
    (mine,) = make_late(place, far, zed, zsum, early[0], stats=stats)
    return near_corr, merge(place, mine, back)


def solution(mesh):
    grid = Mesh(mesh.devices.reshape(8, 8, 4, 2), ("z", "y", "x", "c"))
    axes = ("z", "y", "x", "c")
    return jax.shard_map(
        per_device,
        mesh=grid,
        in_specs=(P(axes, None), P(axes), P(axes)),
        out_specs=(P(axes, None), P(axes, None)),
        check_vma=False,
    )
```

```python
import functools

import jax
import jax.numpy as jnp
from jax import lax
from jax.experimental import pallas as pl
from jax.experimental.pallas import tpu as pltpu
from jax.sharding import Mesh, PartitionSpec as P

HOURS = 4096
SLOTS = 256
COMP_REG = 128
HALF = COMP_REG // 2
EPS = 1e-05
CHUNK = 512
NCHUNK = HOURS // CHUNK
ROWS = 32
MERGE = 64
F32 = jnp.float32
BF16 = jnp.bfloat16
SMEM = pl.BlockSpec(memory_space=pltpu.SMEM)
NT = (((1,), (1,)), ((), ()))


def params(mib):
    return pltpu.CompilerParams(vmem_limit_bytes=mib << 20)


VMEM = pl.BlockSpec(memory_space=pltpu.VMEM)
HBM = pl.BlockSpec(memory_space=pltpu.HBM)


def sum_of(pieces):
    sums = pieces[:4]
    for i, piece in enumerate(pieces[4:]):
        sums[i % 4] = sums[i % 4] + piece
    return (sums[0] + sums[1]) + (sums[2] + sums[3])


def zed_kernel(count, core, ids, x, zed, edge, own, theirs, held, sems):
    steps = SLOTS // ROWS
    rows_of = lambda step: pl.ds(step * ROWS, ROWS)
    copies = [
        pltpu.make_async_copy(x.at[rows_of(step)], held.at[rows_of(step)], sems.at[step]) for step in range(steps)
    ]
    for copy in copies:
        copy.start()
    for step, copy in enumerate(copies):
        copy.wait()
        pieces = [held[rows_of(step), k * 128 : k * 128 + 128].astype(F32) for k in range(HOURS // 128)]
        mean = jnp.sum(sum_of(pieces), axis=1, keepdims=True) * (1.0 / HOURS)
        squares = sum_of([jnp.square(piece - mean) for piece in pieces])
        scale = lax.rsqrt(jnp.sum(squares, axis=1, keepdims=True) * (1.0 / HOURS) + EPS)
        slot = step * ROWS + lax.broadcasted_iota(jnp.int32, (ROWS, 1), 0)
        scale = scale * (slot < count[0]).astype(F32)
        for k in range(HOURS // 256):
            early, late = (((pieces[i] - mean) * scale).astype(BF16) for i in (k, k + HOURS // 256))
            zed[rows_of(step), k * 128 : k * 128 + 128] = early
            zed[rows_of(step), HOURS // 2 + k * 128 : HOURS // 2 + k * 128 + 128] = late
            edge[rows_of(step), k * 128 : k * 128 + 128] = jnp.where(core[0] == 0, early, late)

    index = lax.broadcasted_iota(jnp.int32, (COMP_REG, SLOTS), 0)
    index = (index + HALF * core[0]) & (COMP_REG - 1)
    hot = (ids[...] == index).astype(F32).astype(BF16)
    for k in range(NCHUNK):
        part = jnp.dot(hot, zed[:, k * CHUNK : (k + 1) * CHUNK], preferred_element_type=F32)
        own[k] = part[:HALF]
        theirs[k] = part[HALF:].astype(BF16)


def make_zed(count, core, ids, x):
    block = (NCHUNK, HALF, CHUNK)
    return pl.pallas_call(
        zed_kernel,
        in_specs=[SMEM, SMEM, VMEM, HBM],
        out_specs=[VMEM] * 4,
        out_shape=[
            jax.ShapeDtypeStruct((SLOTS, HOURS), BF16),
            jax.ShapeDtypeStruct((SLOTS, HOURS // 2), BF16),
            jax.ShapeDtypeStruct(block, F32),
            jax.ShapeDtypeStruct(block, BF16),
        ],
        scratch_shapes=[pltpu.VMEM((SLOTS, HOURS), BF16), pltpu.SemaphoreType.DMA((SLOTS // ROWS,))],
        compiler_params=params(48),
        cost_estimate=pl.CostEstimate(flops=300_000_000, bytes_accessed=6 << 20, transcendentals=0),
        name="normalize_and_sum",
    )(count, core, ids, x)


def lane_sums(block):
    wide = block[:, :128]
    for k in range(1, block.shape[1] // 128):
        wide = wide + block[:, k * 128 : (k + 1) * 128]
    return wide


def row_sums(rows, out):
    wide = lane_sums(rows[:, :CHUNK].astype(F32))
    for k in range(1, NCHUNK):
        wide = wide + lane_sums(rows[:, k * CHUNK : (k + 1) * CHUNK].astype(F32))
    out[...] = jnp.broadcast_to(jnp.sum(wide, axis=1, keepdims=True), out.shape)


def edge_kernel(core, zed, halo, mine, theirs, zsum):
    def products(half):
        mine[...] = times(half, halo[...])
        theirs[...] = times(halo[...], half).astype(BF16)

    pl.when(core[0] == 0)(lambda: products(zed[:, HOURS // 2 :]))
    pl.when(core[0] != 0)(lambda: products(zed[:, : HOURS // 2]))
    row_sums(zed, zsum)


def make_edge(place, zed, halo):
    return pl.pallas_call(
        edge_kernel,
        in_specs=[SMEM, VMEM, VMEM],
        out_specs=[VMEM] * 3,
        out_shape=[shape(SLOTS, SLOTS), jax.ShapeDtypeStruct((SLOTS, SLOTS), BF16), shape(SLOTS, 128)],
        compiler_params=params(16),
        cost_estimate=pl.CostEstimate(flops=1 << 29, bytes_accessed=4 << 20, transcendentals=0),
        name="edge_products",
    )(place, zed, halo)


def near_kernel(core, zed, other, mine, got, near, osum, held):
    at = pl.multiple_of(core[0] * SLOTS, SLOTS)
    near[:, pl.ds(at, SLOTS)] = (mine[...] + got[...].astype(F32)) * (1.0 / HOURS)
    near[:, pl.ds(SLOTS - at, SLOTS)] = times(zed[...], other[...]) * (1.0 / HOURS)
    row_sums(other, osum)
    held[...] = other[...]


def make_near(place, zed, other, mine, got):
    return pl.pallas_call(
        near_kernel,
        in_specs=[SMEM] + [VMEM] * 4,
        out_specs=[VMEM] * 3,
        out_shape=[
            shape(SLOTS, 2 * SLOTS),
            shape(SLOTS, 128),
            jax.ShapeDtypeStruct((SLOTS, HOURS), BF16),
        ],
        compiler_params=params(16),
        cost_estimate=pl.CostEstimate(flops=1 << 29, bytes_accessed=5 << 20, transcendentals=0),
        name="neighbour_correlation",
    )(place, zed, other, mine, got)


COMPS = 8 * HALF


def whole(block):
    return block[...].reshape(COMPS, CHUNK)


def hours_of(at, delta):
    return pl.ds(pl.multiple_of(((at + delta) & 7) * CHUNK, CHUNK), CHUNK)


def times(left, right):
    return lax.dot_general(left, right, NT, preferred_element_type=F32)


def early_kernel(place, *refs):
    blocks, (zed, other, mine, theirs, s_1, s_2) = refs[:7], refs[7:]
    core, at = place[0], place[1]

    def add(hours, rows, start):
        wide = rows.astype(F32)
        for out, new in (
            (mine, times(zed[:, hours], rows)),
            (theirs, times(other[:, hours], rows)),
            (s_1, lane_sums(wide)),
            (s_2, lane_sums(wide * wide)),
        ):
            out[...] = new if start else out[...] + new

    @pl.when(core == 0)
    def _():
        for i, (block, delta) in enumerate(zip(blocks, (0, 7, 1, 6, 2, 5, 3))):
            add(hours_of(at, delta), whole(block), i == 0)

    @pl.when(core != 0)
    def _():
        for k in range(NCHUNK):
            rows = jnp.concatenate([block[k] for block in blocks] + [blocks[0][k]], axis=0)
            add(slice(k * CHUNK, (k + 1) * CHUNK), rows, k == 0)


def late_kernel(here, place, far, zed, zsum, acc, *refs):
    core, at = place[0], place[1]
    last = slice(COMPS - HALF, COMPS)
    if here:
        e_1, e_2, out, stats, s_1, s_2 = refs
        s_1[...], s_2[...] = e_1[...], e_2[...]
    else:
        stats, out = refs

    @pl.when(core == 0)
    def _():
        rows = whole(far)
        out[...] = acc[...] + times(zed[:, hours_of(at, 4)], rows)
        if here:
            wide = rows.astype(F32)
            s_1[...] += lane_sums(wide)
            s_2[...] += lane_sums(wide * wide)

    @pl.when(core != 0)
    def _():
        total = jnp.zeros((SLOTS, 128), F32)
        wide_1 = wide_2 = jnp.zeros((HALF, 128), F32)
        for k in range(NCHUNK):
            rows = far[k]
            total = total + times(zed[:, k * CHUNK : (k + 1) * CHUNK], jnp.concatenate([rows, rows], axis=0))
            if here:
                wide = rows.astype(F32)
                wide_1, wide_2 = wide_1 + lane_sums(wide), wide_2 + lane_sums(wide * wide)
        if here:
            s_1[last], s_2[last] = wide_1, wide_2
        out[:, : COMPS - 128] = acc[:, : COMPS - 128]
        first = lax.broadcasted_iota(jnp.int32, (SLOTS, 128), 1) < HALF
        out[:, COMPS - 128 :] = jnp.where(first, acc[:, COMPS - 128 :], total)

    if here:
        mean = jnp.sum(s_1[...].T, axis=0, keepdims=True) * (1.0 / HOURS)
        square = jnp.sum(s_2[...].T, axis=0, keepdims=True) * (1.0 / HOURS)
        inv = lax.rsqrt(jnp.maximum(square - mean * mean, 0.0) + EPS) * (1.0 / HOURS)
        stats[0:8, :] = jnp.broadcast_to(mean, (8, COMPS))
        stats[8:16, :] = jnp.broadcast_to(inv, (8, COMPS))
    else:
        mean = stats[0:1, :]
        inv = stats[8:9, :]
    out[...] = (out[...] - zsum[:, 0:1] * mean) * inv


def shape(*dims):
    return jax.ShapeDtypeStruct(dims, F32)


def make_early(place, blocks, zed, other):
    return pl.pallas_call(
        early_kernel,
        in_specs=[SMEM] + [VMEM] * 9,
        out_specs=[VMEM] * 4,
        out_shape=[shape(SLOTS, COMPS)] * 2 + [shape(COMPS, 128)] * 2,
        compiler_params=params(24),
        cost_estimate=pl.CostEstimate(flops=15 << 27, bytes_accessed=9 << 20, transcendentals=0),
        name="early_composites",
    )(place, *blocks, zed, other)


def make_late(place, far, zed, zsum, acc, sums=None, stats=None):
    here = stats is None
    scratch = [pltpu.VMEM((COMPS, 128), F32)] * 2 if here else []
    extra = list(sums) if here else [stats]
    return pl.pallas_call(
        functools.partial(late_kernel, here),
        in_specs=[SMEM] + [VMEM] * (4 + len(extra)),
        out_specs=[VMEM] * (2 if here else 1),
        out_shape=[shape(SLOTS, COMPS)] + ([shape(16, COMPS)] if here else []),
        scratch_shapes=scratch,
        compiler_params=params(24),
        cost_estimate=pl.CostEstimate(flops=1 << 27, bytes_accessed=4 << 20, transcendentals=0),
        name="late_composites",
    )(place, far, zed, zsum, acc, *extra)


def merge_kernel(place, mine, got, out, held, sems):
    core, z = place[0], place[2]
    first = lax.broadcasted_iota(jnp.int32, (MERGE, 128), 1) < HALF
    copies = []
    for r in range(SLOTS // MERGE):
        rows = slice(r * MERGE, (r + 1) * MERGE)
        for to in range(8):
            tile = slice(to // 2 * 128, to // 2 * 128 + 128)
            low = jnp.where(core == 0, mine[rows, tile], got[rows, tile])
            d = (to - z) & 7
            slot = jnp.where(d == 0, 0, jnp.where(d == 4, 7, jnp.where(d < 4, 2 * d, 15 - 2 * d)))
            tile = pl.ds(pl.multiple_of((slot >> 1) * 128, 128), 128)
            high = jnp.where(core == 0, got[rows, tile], mine[rows, tile])
            high = jnp.where((slot & 1) == 1, high, pltpu.roll(high, HALF, 1))
            low = pltpu.roll(low, HALF, 1) if to % 2 else low
            held[rows, to * 128 : to * 128 + 128] = jnp.where(first, low, high)
        copies.append(pltpu.make_async_copy(held.at[rows], out.at[rows], sems.at[r]))
        copies[-1].start()
    for copy in copies:
        copy.wait()


def merge(place, mine, got):
    return pl.pallas_call(
        merge_kernel,
        in_specs=[SMEM, VMEM, VMEM],
        out_specs=pl.BlockSpec(memory_space=pl.ANY),
        out_shape=shape(SLOTS, 1024),
        scratch_shapes=[pltpu.VMEM((SLOTS, 1024), F32), pltpu.SemaphoreType.DMA((SLOTS // MERGE,))],
        compiler_params=params(8),
        cost_estimate=pl.CostEstimate(flops=1 << 20, bytes_accessed=2 << 20, transcendentals=0),
        name="merge_halves",
    )(place, mine, got)


def spread_kernel(blocks, out):
    total = blocks[0].astype(F32)
    for i in range(1, 32):
        total = total + blocks[i].astype(F32)
    rows = total.astype(BF16)
    for i in range(32):
        out[i] = rows


def sum_and_spread(blocks):
    return pl.pallas_call(
        spread_kernel,
        in_specs=[VMEM],
        out_specs=VMEM,
        out_shape=jax.ShapeDtypeStruct(blocks.shape, BF16),
        compiler_params=params(8),
        cost_estimate=pl.CostEstimate(flops=1 << 18, bytes_accessed=1 << 20, transcendentals=0),
        name="sum_and_spread",
    )(blocks)


def groups_and_rings():
    number = lambda z, y, x, c: ((z * 8 + y) * 4 + x) * 2 + c
    line = [(i, x) for i in range(8) for x in range(4)]
    groups = [[number(z, y, x, 0) for z, x in line] for y in range(8)]
    groups += [[number(z, y, x, 1) for y, x in line] for z in range(8)]
    up = []
    for z in range(8):
        for y in range(8):
            for x in range(4):
                up.append((number(z, y, x, 0), number(z, (y + 1) % 8, x, 0)))
                up.append((number(z, y, x, 1), number((z + 1) % 8, y, x, 1)))
    return groups, up, [(j, i) for i, j in up]


def per_device(anomalies, station_count, composite_of):
    core, y, z = (lax.axis_index(name).astype(jnp.int32) for name in ("c", "y", "z"))
    place = jnp.stack([core, jnp.where(core == 0, y, z), z])
    swap = [(0, 1), (1, 0)]
    every = ("z", "y", "x", "c")
    together = lax.optimization_barrier
    groups, up, down = groups_and_rings()
    step_up = dict(up)
    up_2 = [(i, step_up[j]) for i, j in up]
    down_2 = [(j, i) for i, j in up_2]
    zed, edge, own, theirs = make_zed(station_count, place, composite_of.reshape(1, SLOTS), anomalies)

    got = lax.ppermute(theirs, "c", swap)
    part = (own + got.astype(F32)).astype(BF16).reshape(32, 16, CHUNK)
    part, edge = together((part, edge))
    across = [(i, i + 1) for i in range(1, 63, 2)]
    across += [(j, i) for i, j in across]
    halo = lax.ppermute(edge, every[1:], across)
    blocks = lax.all_to_all(part, ("y", "x"), split_axis=0, concat_axis=0, tiled=True)
    spread = sum_and_spread(blocks)

    near_mine, near_theirs, zsum = make_edge(place, zed, halo)
    near_got = lax.ppermute(near_theirs, every[1:], across)
    first = lax.all_to_all(spread, every, split_axis=0, concat_axis=0, axis_index_groups=groups, tiled=True)
    first, near_got, zed = together((first.reshape(8, HALF, CHUNK), near_got, zed))
    other = lax.ppermute(zed, "c", swap)

    near_1, near_2, far_1, far_2 = (lax.ppermute(first, every, ring) for ring in (up, down, up_2, down_2))
    above = [first, near_1, far_1, lax.ppermute(far_1, every, up)]
    far = lax.ppermute(far_1, every, up_2)
    below = [first, near_2, far_2, lax.ppermute(far_2, every, down)]
    near_corr, osum, other = make_near(place, zed, other, near_mine, near_got)

    blocks = [first, above[1], below[1], above[2], below[2], above[3], below[3]]
    early = make_early(place, blocks, zed, other)
    for_other, stats = make_late(place, far, other, osum, early[1], sums=early[2:])
    back = lax.ppermute(for_other, "c", swap)
    (mine,) = make_late(place, far, zed, zsum, early[0], stats=stats)
    return near_corr, merge(place, mine, back)


def solution(mesh):
    grid = Mesh(mesh.devices.reshape(8, 8, 4, 2), ("z", "y", "x", "c"))
    axes = ("z", "y", "x", "c")
    return jax.shard_map(
        per_device,
        mesh=grid,
        in_specs=(P(axes, None), P(axes), P(axes)),
        out_specs=(P(axes, None), P(axes, None)),
        check_vma=False,
    )
```

```python
import functools

import jax
import jax.numpy as jnp
from jax import lax
from jax.experimental import pallas as pl
from jax.experimental.pallas import tpu as pltpu
from jax.sharding import Mesh, PartitionSpec as P

HOURS = 4096
SLOTS = 256
COMP_REG = 128
HALF = COMP_REG // 2
EPS = 1e-05
CHUNK = 512
NCHUNK = HOURS // CHUNK
ROWS = 32
MERGE = 64
F32 = jnp.float32
BF16 = jnp.bfloat16
SMEM = pl.BlockSpec(memory_space=pltpu.SMEM)
NT = (((1,), (1,)), ((), ()))


def params(mib):
    return pltpu.CompilerParams(vmem_limit_bytes=mib << 20)


VMEM = pl.BlockSpec(memory_space=pltpu.VMEM)
HBM = pl.BlockSpec(memory_space=pltpu.HBM)


def sum_of(pieces):
    sums = pieces[:4]
    for i, piece in enumerate(pieces[4:]):
        sums[i % 4] = sums[i % 4] + piece
    return (sums[0] + sums[1]) + (sums[2] + sums[3])


def zed_kernel(count, core, ids, x, zed, edge, own, theirs, held, sems):
    steps = SLOTS // ROWS
    rows_of = lambda step: pl.ds(step * ROWS, ROWS)
    copies = [
        pltpu.make_async_copy(x.at[rows_of(step)], held.at[rows_of(step)], sems.at[step]) for step in range(steps)
    ]
    for copy in copies:
        copy.start()
    for step, copy in enumerate(copies):
        copy.wait()
        pieces = [held[rows_of(step), k * 128 : k * 128 + 128].astype(F32) for k in range(HOURS // 128)]
        mean = jnp.sum(sum_of(pieces), axis=1, keepdims=True) * (1.0 / HOURS)
        squares = sum_of([jnp.square(piece - mean) for piece in pieces])
        scale = lax.rsqrt(jnp.sum(squares, axis=1, keepdims=True) * (1.0 / HOURS) + EPS)
        slot = step * ROWS + lax.broadcasted_iota(jnp.int32, (ROWS, 1), 0)
        scale = scale * (slot < count[0]).astype(F32)
        for k in range(HOURS // 256):
            early, late = (((pieces[i] - mean) * scale).astype(BF16) for i in (k, k + HOURS // 256))
            zed[rows_of(step), k * 128 : k * 128 + 128] = early
            zed[rows_of(step), HOURS // 2 + k * 128 : HOURS // 2 + k * 128 + 128] = late
            edge[rows_of(step), k * 128 : k * 128 + 128] = jnp.where(core[0] == 0, early, late)

    index = lax.broadcasted_iota(jnp.int32, (COMP_REG, SLOTS), 0)
    index = (index + HALF * core[0]) & (COMP_REG - 1)
    hot = (ids[...] == index).astype(F32).astype(BF16)
    for k in range(NCHUNK):
        part = jnp.dot(hot, zed[:, k * CHUNK : (k + 1) * CHUNK], preferred_element_type=F32)
        own[k] = part[:HALF]
        theirs[k] = part[HALF:].astype(BF16)


def make_zed(count, core, ids, x):
    block = (NCHUNK, HALF, CHUNK)
    return pl.pallas_call(
        zed_kernel,
        in_specs=[SMEM, SMEM, VMEM, HBM],
        out_specs=[VMEM] * 4,
        out_shape=[
            jax.ShapeDtypeStruct((SLOTS, HOURS), BF16),
            jax.ShapeDtypeStruct((SLOTS, HOURS // 2), BF16),
            jax.ShapeDtypeStruct(block, F32),
            jax.ShapeDtypeStruct(block, BF16),
        ],
        scratch_shapes=[pltpu.VMEM((SLOTS, HOURS), BF16), pltpu.SemaphoreType.DMA((SLOTS // ROWS,))],
        compiler_params=params(48),
        cost_estimate=pl.CostEstimate(flops=300_000_000, bytes_accessed=6 << 20, transcendentals=0),
        name="normalize_and_sum",
    )(count, core, ids, x)


def lane_sums(block):
    wide = block[:, :128]
    for k in range(1, block.shape[1] // 128):
        wide = wide + block[:, k * 128 : (k + 1) * 128]
    return wide


def row_sums(rows, out):
    wide = lane_sums(rows[:, :CHUNK].astype(F32))
    for k in range(1, NCHUNK):
        wide = wide + lane_sums(rows[:, k * CHUNK : (k + 1) * CHUNK].astype(F32))
    out[...] = jnp.broadcast_to(jnp.sum(wide, axis=1, keepdims=True), out.shape)


def edge_kernel(core, zed, halo, mine, theirs, zsum):
    def products(half):
        mine[...] = times(half, halo[...])
        theirs[...] = times(halo[...], half).astype(BF16)

    pl.when(core[0] == 0)(lambda: products(zed[:, HOURS // 2 :]))
    pl.when(core[0] != 0)(lambda: products(zed[:, : HOURS // 2]))
    row_sums(zed, zsum)


def make_edge(place, zed, halo):
    return pl.pallas_call(
        edge_kernel,
        in_specs=[SMEM, VMEM, VMEM],
        out_specs=[VMEM] * 3,
        out_shape=[shape(SLOTS, SLOTS), jax.ShapeDtypeStruct((SLOTS, SLOTS), BF16), shape(SLOTS, 128)],
        compiler_params=params(16),
        cost_estimate=pl.CostEstimate(flops=1 << 29, bytes_accessed=4 << 20, transcendentals=0),
        name="edge_products",
    )(place, zed, halo)


def near_kernel(core, zed, other, mine, got, near, osum, held):
    at = pl.multiple_of(core[0] * SLOTS, SLOTS)
    near[:, pl.ds(at, SLOTS)] = (mine[...] + got[...].astype(F32)) * (1.0 / HOURS)
    near[:, pl.ds(SLOTS - at, SLOTS)] = times(zed[...], other[...]) * (1.0 / HOURS)
    row_sums(other, osum)
    held[...] = other[...]


def make_near(place, zed, other, mine, got):
    return pl.pallas_call(
        near_kernel,
        in_specs=[SMEM] + [VMEM] * 4,
        out_specs=[VMEM] * 3,
        out_shape=[
            shape(SLOTS, 2 * SLOTS),
            shape(SLOTS, 128),
            jax.ShapeDtypeStruct((SLOTS, HOURS), BF16),
        ],
        compiler_params=params(16),
        cost_estimate=pl.CostEstimate(flops=1 << 29, bytes_accessed=5 << 20, transcendentals=0),
        name="neighbour_correlation",
    )(place, zed, other, mine, got)


COMPS = 8 * HALF


def whole(block):
    return block[...].reshape(COMPS, CHUNK)


def hours_of(at, delta):
    return pl.ds(pl.multiple_of(((at + delta) & 7) * CHUNK, CHUNK), CHUNK)


def times(left, right):
    return lax.dot_general(left, right, NT, preferred_element_type=F32)


def early_kernel(place, *refs):
    blocks, (zed, other, mine, theirs, s_1, s_2) = refs[:7], refs[7:]
    core, at = place[0], place[1]

    def add(hours, rows, start):
        wide = rows.astype(F32)
        for out, new in (
            (mine, times(zed[:, hours], rows)),
            (theirs, times(other[:, hours], rows)),
            (s_1, lane_sums(wide)),
            (s_2, lane_sums(wide * wide)),
        ):
            out[...] = new if start else out[...] + new

    @pl.when(core == 0)
    def _():
        for i, (block, delta) in enumerate(zip(blocks, (0, 7, 1, 6, 2, 5, 3))):
            add(hours_of(at, delta), whole(block), i == 0)

    @pl.when(core != 0)
    def _():
        for k in range(NCHUNK):
            rows = jnp.concatenate([block[k] for block in blocks] + [blocks[0][k]], axis=0)
            add(slice(k * CHUNK, (k + 1) * CHUNK), rows, k == 0)


def late_kernel(here, place, far_a, far_b, zed, zsum, acc, *refs):
    core, at = place[0], place[1]
    last = slice(COMPS - HALF, COMPS)
    if here:
        e_1, e_2, out, stats, s_1, s_2 = refs
        s_1[...], s_2[...] = e_1[...], e_2[...]
    else:
        stats, out = refs

    @pl.when(core == 0)
    def _():
        rows = jnp.concatenate([far_a[...], far_b[...]], axis=0).reshape(COMPS, CHUNK)
        out[...] = acc[...] + times(zed[:, hours_of(at, 4)], rows)
        if here:
            wide = rows.astype(F32)
            s_1[...] += lane_sums(wide)
            s_2[...] += lane_sums(wide * wide)

    @pl.when(core != 0)
    def _():
        total = jnp.zeros((SLOTS, 128), F32)
        wide_1 = wide_2 = jnp.zeros((HALF, 128), F32)
        for k in range(NCHUNK):
            rows = far_a[k] if k < 4 else far_b[k - 4]
            total = total + times(zed[:, k * CHUNK : (k + 1) * CHUNK], jnp.concatenate([rows, rows], axis=0))
            if here:
                wide = rows.astype(F32)
                wide_1, wide_2 = wide_1 + lane_sums(wide), wide_2 + lane_sums(wide * wide)
        if here:
            s_1[last], s_2[last] = wide_1, wide_2
        out[:, : COMPS - 128] = acc[:, : COMPS - 128]
        first = lax.broadcasted_iota(jnp.int32, (SLOTS, 128), 1) < HALF
        out[:, COMPS - 128 :] = jnp.where(first, acc[:, COMPS - 128 :], total)

    if here:
        mean = jnp.sum(s_1[...].T, axis=0, keepdims=True) * (1.0 / HOURS)
        square = jnp.sum(s_2[...].T, axis=0, keepdims=True) * (1.0 / HOURS)
        inv = lax.rsqrt(jnp.maximum(square - mean * mean, 0.0) + EPS) * (1.0 / HOURS)
        stats[0:8, :] = jnp.broadcast_to(mean, (8, COMPS))
        stats[8:16, :] = jnp.broadcast_to(inv, (8, COMPS))
    else:
        mean = stats[0:1, :]
        inv = stats[8:9, :]
    out[...] = (out[...] - zsum[:, 0:1] * mean) * inv


def shape(*dims):
    return jax.ShapeDtypeStruct(dims, F32)


def make_early(place, blocks, zed, other):
    return pl.pallas_call(
        early_kernel,
        in_specs=[SMEM] + [VMEM] * 9,
        out_specs=[VMEM] * 4,
        out_shape=[shape(SLOTS, COMPS)] * 2 + [shape(COMPS, 128)] * 2,
        compiler_params=params(24),
        cost_estimate=pl.CostEstimate(flops=15 << 27, bytes_accessed=9 << 20, transcendentals=0),
        name="early_composites",
    )(place, *blocks, zed, other)


def make_late(place, far, zed, zsum, acc, sums=None, stats=None):
    here = stats is None
    scratch = [pltpu.VMEM((COMPS, 128), F32)] * 2 if here else []
    extra = list(sums) if here else [stats]
    return pl.pallas_call(
        functools.partial(late_kernel, here),
        in_specs=[SMEM] + [VMEM] * (5 + len(extra)),
        out_specs=[VMEM] * (2 if here else 1),
        out_shape=[shape(SLOTS, COMPS)] + ([shape(16, COMPS)] if here else []),
        scratch_shapes=scratch,
        compiler_params=params(24),
        cost_estimate=pl.CostEstimate(flops=1 << 27, bytes_accessed=4 << 20, transcendentals=0),
        name="late_composites",
    )(place, *far, zed, zsum, acc, *extra)


def merge_kernel(place, mine, got, out, held, sems):
    core, z = place[0], place[2]
    first = lax.broadcasted_iota(jnp.int32, (MERGE, 128), 1) < HALF
    copies = []
    for r in range(SLOTS // MERGE):
        rows = slice(r * MERGE, (r + 1) * MERGE)
        for to in range(8):
            tile = slice(to // 2 * 128, to // 2 * 128 + 128)
            low = jnp.where(core == 0, mine[rows, tile], got[rows, tile])
            d = (to - z) & 7
            slot = jnp.where(d == 0, 0, jnp.where(d == 4, 7, jnp.where(d < 4, 2 * d, 15 - 2 * d)))
            tile = pl.ds(pl.multiple_of((slot >> 1) * 128, 128), 128)
            high = jnp.where(core == 0, got[rows, tile], mine[rows, tile])
            high = jnp.where((slot & 1) == 1, high, pltpu.roll(high, HALF, 1))
            low = pltpu.roll(low, HALF, 1) if to % 2 else low
            held[rows, to * 128 : to * 128 + 128] = jnp.where(first, low, high)
        copies.append(pltpu.make_async_copy(held.at[rows], out.at[rows], sems.at[r]))
        copies[-1].start()
    for copy in copies:
        copy.wait()


def merge(place, mine, got):
    return pl.pallas_call(
        merge_kernel,
        in_specs=[SMEM, VMEM, VMEM],
        out_specs=pl.BlockSpec(memory_space=pl.ANY),
        out_shape=shape(SLOTS, 1024),
        scratch_shapes=[pltpu.VMEM((SLOTS, 1024), F32), pltpu.SemaphoreType.DMA((SLOTS // MERGE,))],
        compiler_params=params(8),
        cost_estimate=pl.CostEstimate(flops=1 << 20, bytes_accessed=2 << 20, transcendentals=0),
        name="merge_halves",
    )(place, mine, got)


def spread_kernel(blocks, out):
    total = blocks[0].astype(F32)
    for i in range(1, 32):
        total = total + blocks[i].astype(F32)
    rows = total.astype(BF16)
    for i in range(32):
        out[i] = rows


def sum_and_spread(blocks):
    return pl.pallas_call(
        spread_kernel,
        in_specs=[VMEM],
        out_specs=VMEM,
        out_shape=jax.ShapeDtypeStruct(blocks.shape, BF16),
        compiler_params=params(8),
        cost_estimate=pl.CostEstimate(flops=1 << 18, bytes_accessed=1 << 20, transcendentals=0),
        name="sum_and_spread",
    )(blocks)


def groups_and_rings():
    number = lambda z, y, x, c: ((z * 8 + y) * 4 + x) * 2 + c
    line = [(i, x) for i in range(8) for x in range(4)]
    groups = [[number(z, y, x, 0) for z, x in line] for y in range(8)]
    groups += [[number(z, y, x, 1) for y, x in line] for z in range(8)]
    up = []
    for z in range(8):
        for y in range(8):
            for x in range(4):
                up.append((number(z, y, x, 0), number(z, (y + 1) % 8, x, 0)))
                up.append((number(z, y, x, 1), number((z + 1) % 8, y, x, 1)))
    return groups, up, [(j, i) for i, j in up]


def per_device(anomalies, station_count, composite_of):
    core, y, z = (lax.axis_index(name).astype(jnp.int32) for name in ("c", "y", "z"))
    place = jnp.stack([core, jnp.where(core == 0, y, z), z])
    swap = [(0, 1), (1, 0)]
    every = ("z", "y", "x", "c")
    together = lax.optimization_barrier
    groups, up, down = groups_and_rings()
    step_up = dict(up)
    up_2 = [(i, step_up[j]) for i, j in up]
    down_2 = [(j, i) for i, j in up_2]
    zed, edge, own, theirs = make_zed(station_count, place, composite_of.reshape(1, SLOTS), anomalies)

    got = lax.ppermute(theirs, "c", swap)
    part = (own + got.astype(F32)).astype(BF16).reshape(32, 16, CHUNK)
    part, edge = together((part, edge))
    across = [(i, i + 1) for i in range(1, 63, 2)]
    across += [(j, i) for i, j in across]
    halo = lax.ppermute(edge, every[1:], across)
    blocks = lax.all_to_all(part, ("y", "x"), split_axis=0, concat_axis=0, tiled=True)
    spread = sum_and_spread(blocks)

    near_mine, near_theirs, zsum = make_edge(place, zed, halo)
    near_got = lax.ppermute(near_theirs, every[1:], across)
    first = lax.all_to_all(spread, every, split_axis=0, concat_axis=0, axis_index_groups=groups, tiled=True)
    first, near_got, zed = together((first.reshape(8, HALF, CHUNK), near_got, zed))
    other = lax.ppermute(zed, "c", swap)

    near_1, near_2, far_1, far_2 = (lax.ppermute(first, every, ring) for ring in (up, down, up_2, down_2))
    above = [first, near_1, far_1, lax.ppermute(far_1, every, up)]
    far = lax.ppermute(far_1[:4], every, up_2), lax.ppermute(far_2[4:], every, down_2)
    below = [first, near_2, far_2, lax.ppermute(far_2, every, down)]
    near_corr, osum, other = make_near(place, zed, other, near_mine, near_got)

    blocks = [first, above[1], below[1], above[2], below[2], above[3], below[3]]
    early = make_early(place, blocks, zed, other)
    for_other, stats = make_late(place, far, other, osum, early[1], sums=early[2:])
    back = lax.ppermute(for_other, "c", swap)
    (mine,) = make_late(place, far, zed, zsum, early[0], stats=stats)
    return near_corr, merge(place, mine, back)


def solution(mesh):
    grid = Mesh(mesh.devices.reshape(8, 8, 4, 2), ("z", "y", "x", "c"))
    axes = ("z", "y", "x", "c")
    return jax.shard_map(
        per_device,
        mesh=grid,
        in_specs=(P(axes, None), P(axes), P(axes)),
        out_specs=(P(axes, None), P(axes, None)),
        check_vma=False,
    )
```
